512 devices in a mesh: seq: 16 (over y, x), blk: 16 (over z_lo, core), cfg: 2 (over z_hi).
Axes of the slice: x: 4, y: 4, z: 16 (z_hi: 2, z_lo: 8; z = z_hi * 8 + z_lo), core: 2. Of those that a mesh axis runs over, the one named last changes fastest.
Arguments:
- queries: bfloat16 [2, 8192, 4096], P('cfg', ('seq', 'blk')), may hold values from -6 to 6
- keys: bfloat16 [2, 8192, 4096], P('cfg', ('seq', 'blk')), may hold values from -6 to 6
- values: bfloat16 [2, 8192, 4096], P('cfg', ('seq', 'blk')), may hold values from -6 to 6
- head_weight: bfloat16 [4096, 64], replicated, may hold values from -0.09375 to 0.09375
- noisy_latent: float32 [16, 32, 64, 16], P('seq', 'blk', 'cfg'), may hold values from -6 to 6
- noise_level: float32 [1], replicated, may hold values from 0.3 to 1
- conv_weight: bfloat16 [3, 3, 3, 16, 384], replicated, may hold values from -0.3125 to 0.3125
Outputs:
- clean_latent: float32 [16, 32, 64, 16], P('seq', 'blk', 'cfg')
- decoded: bfloat16 [16, 32, 64, 384], P('seq', 'blk', 'cfg')
The draws below stay inside these ranges and needn't reach their ends.
All inputs are finite; a program needn't handle non-finite values.
Results may differ from the reference program's by a relative error of at most 0.013.
Values may be sent and summed in bfloat16 or wider, within the bound.
A program may use at most 64 MiB of HBM per device.

```python
import math
import jax
import jax.numpy as jnp
from jax import lax

HEADS = 32
HEAD_DIM = 128
LAT_CH = 16
OUT_CH = 384
FEAT = 4096
PATCH_OUT = 64
TOKENS = 8192
FRAMES = 16
LAT_ROWS = 32
LAT_COLS = 64


def draw_queries(key, part):
    key = jax.random.fold_in(key, 11)
    base = jnp.clip(1.6 * jax.random.normal(key, (2, TOKENS, FEAT), jnp.float32), -6.0, 6.0)
    return base.astype(jnp.bfloat16)


def draw_keys(key, part):
    key = jax.random.fold_in(key, 23)
    base = jnp.clip(1.6 * jax.random.normal(key, (2, TOKENS, FEAT), jnp.float32), -6.0, 6.0)
    return base.astype(jnp.bfloat16)


def level_of(own_key, extent, shards, least, top_value):
    gain = 1.0
    for axis_at, parts in shards:
        heights = jax.random.uniform(jax.random.fold_in(jax.random.fold_in(own_key, 6), axis_at), (parts,), jnp.float32, least / len(shards), top_value / len(shards))
        gain = gain * jnp.repeat(jnp.exp(heights), extent[axis_at] // parts).reshape((-1,) + (1,) * (len(extent) - 1 - axis_at))
    return gain


def noise(rng, dims, spread, most, shards=(), dtype=jnp.bfloat16):
    drawn = jax.random.normal(rng, dims, jnp.float32) * spread
    if len(shards) > 0:
        drawn = level_of(rng, dims, shards, -0.22, 0.18) * drawn
    return jnp.clip(drawn, min=-most, max=most).astype(dtype)


def setup_inputs(seed: int = 0) -> dict:
    key_of = jax.random.split(jax.random.key(seed), 8)
    return {
        "queries": draw_queries(jax.random.fold_in(key_of[7], 71), 0),
        "keys": draw_keys(jax.random.fold_in(key_of[7], 71), 0),
        "values": noise(key_of[2], (2, TOKENS, FEAT), 1.0, 6.0, ((0, 2), (1, 256))),
        "head_weight": noise(key_of[3], (FEAT, PATCH_OUT), FEAT ** -0.5, 0.09375),
        "noisy_latent": noise(key_of[4], (FRAMES, LAT_ROWS, LAT_COLS, LAT_CH), 1.0, 6.0, ((0, 16), (1, 16), (2, 2)), jnp.float32),
        "noise_level": jnp.clip(jax.random.uniform(key_of[5], (1,), jnp.float32, 0.3, 1.0), 0.3, 1.0),
        "conv_weight": noise(key_of[6], (3, 3, 3, LAT_CH, OUT_CH), (27 * LAT_CH) ** -0.5, 0.3125),
    }


guide_scale = 5.0
norm_eps = 1e-06

def reference(queries, keys, values, head_weight, noisy_latent, noise_level, conv_weight):
    scale = HEAD_DIM ** (-0.5)
    block = math.gcd(TOKENS, 1024)

    def split_heads(tensor):
        return tensor.reshape(2, TOKENS, HEADS, HEAD_DIM).transpose(0, 2, 1, 3).reshape(2 * HEADS, TOKENS, HEAD_DIM)

    def one_head(triple):
        query, key_rows, value_rows = triple
        key_full = key_rows.astype(jnp.float32)
        value_full = value_rows.astype(jnp.float32)

        def one_block(query_block):
            scores = jnp.dot(query_block.astype(jnp.float32), key_full.T) * scale
            largest = lax.optimization_barrier(jnp.max(scores, axis=1, keepdims=True))
            probs = jnp.exp(scores - largest)
            total = lax.optimization_barrier(jnp.sum(probs, axis=1, keepdims=True))
            rounded = lax.optimization_barrier(probs.astype(jnp.bfloat16))
            mixed = jnp.dot(rounded.astype(jnp.float32), value_full)
            return (mixed / total).astype(jnp.bfloat16)
        blocks = lax.map(one_block, query.reshape(TOKENS // block, block, HEAD_DIM))
        return blocks.reshape(TOKENS, HEAD_DIM)
    attended = lax.map(one_head, (split_heads(queries), split_heads(keys), split_heads(values)))
    attended = attended.reshape(2, HEADS, TOKENS, HEAD_DIM).transpose(0, 2, 1, 3).reshape(2, TOKENS, FEAT)
    cond = attended[0].astype(jnp.float32)
    uncond = attended[1].astype(jnp.float32)
    guided = uncond + guide_scale * (cond - uncond)
    velocity = jnp.dot(guided, head_weight.astype(jnp.float32), precision=lax.Precision.HIGHEST)
    motion = velocity.reshape(FRAMES, LAT_ROWS // 2, LAT_COLS // 2, 2, 2, LAT_CH)
    motion = motion.transpose(0, 1, 3, 2, 4, 5).reshape(FRAMES, LAT_ROWS, LAT_COLS, LAT_CH)
    clean_latent = noisy_latent - noise_level[0] * motion
    latent_in = lax.optimization_barrier(clean_latent.astype(jnp.bfloat16))
    padded = jnp.pad(latent_in.astype(jnp.float32), ((2, 0), (1, 1), (1, 1), (0, 0)))
    kernel = conv_weight.astype(jnp.float32)
    summed = jnp.zeros((FRAMES, LAT_ROWS, LAT_COLS, OUT_CH), jnp.float32)
    for offset_f in range(3):
        for offset_r in range(3):
            for offset_c in range(3):
                window = padded[offset_f:offset_f + FRAMES, offset_r:offset_r + LAT_ROWS, offset_c:offset_c + LAT_COLS]
                summed = summed + jnp.einsum('frwc,co->frwo', window, kernel[offset_f, offset_r, offset_c])
    factor = lax.rsqrt(lax.optimization_barrier(jnp.mean(summed * summed, axis=-1, keepdims=True)) + norm_eps)
    decoded = jax.nn.silu(summed * factor).astype(jnp.bfloat16)
    return (clean_latent, decoded)
```

```python
import jax
import jax.numpy as jnp
from jax import lax
from jax.experimental import pallas as pl
from jax.experimental.pallas import tpu as pltpu
from jax.sharding import PartitionSpec as P

F32 = jnp.float32
BF16 = jnp.bfloat16
MESH = pl.DeviceIdType.MESH

guide_scale = 5.0
norm_eps = 1e-06
LOG_SCALE = float(128 ** (-0.5) * 1.4426950408889634)

NX = 4
NY = 4
NZ = 8
HEADS = 32
ROWS = 32
KV_ROWS = 48
V_ROWS = 80


def kernel(
    q_ref, k_ref, v_ref, w_ref, noisy_ref, level_ref, cw_ref,
    clean_ref, decoded_ref,
    send_kv, send_q, rkv, rq, vt, c1s, c1r, c2s, c2r, halo, ext, patches, moved,
    s_kv, s_q, r_kv, r_q, s_b1, r_b1, s_b2, r_b2, s_core, r_core,
    s_c1, r_c1, s_c2, r_c2, s_halo, r_halo,
):
    seq = lax.axis_index("seq")
    blk = lax.axis_index("blk")
    cfg = lax.axis_index("cfg")
    y, x = seq // NX, seq % NX
    z, core = blk // 2, blk % 2
    half, zl = z // 4, z % 4

    def from_plane(i):
        return ((half + i % 2) % 2) * 4 + (zl + 4 - i // 2) % 4

    def to_plane(i):
        return ((half + i % 2) % 2) * 4 + (zl + i // 2) % 4

    def group(yy, zz):
        return (yy * NX + x, zz * 2 + core, cfg)

    right = (y * NX + (x + 1) % NX, blk, cfg)
    left = (y * NX + (x + 3) % NX, blk, cfg)
    sibling = (seq, z * 2 + 1 - core, cfg)

    halo[...] = jnp.zeros_like(halo)
    ext[...] = jnp.zeros_like(ext)

    barrier = pltpu.get_barrier_semaphore()

    def greet(i, carry):
        zz, yy = to_plane(i // 4), (y + i % 4) % 4
        pl.semaphore_signal(barrier, inc=1, device_id=group(yy, zz), device_id_type=MESH)
        return carry

    lax.fori_loop(1, HEADS, greet, 0)
    for other in (right, left, sibling):
        pl.semaphore_signal(barrier, inc=1, device_id=other, device_id_type=MESH)

    def greet_branch(i, carry):
        pl.semaphore_signal(
            barrier, inc=1, device_id=(seq, i * 2 + core, 1 - cfg), device_id_type=MESH
        )
        return carry

    lax.fori_loop(0, NZ, greet_branch, 0)

    for h in range(HEADS):
        cols = slice(h * 128, (h + 1) * 128)
        send_kv[h, 0:32, :] = k_ref[:, cols]
        send_q[h] = q_ref[:, cols]
        vp = jnp.dot(v_ref[:, cols], w_ref[cols, :], preferred_element_type=F32)
        send_kv[h, 32:48, :] = jnp.concatenate([vp[0:16], vp[16:32]], axis=1).astype(BF16)

    pl.semaphore_wait(barrier, HEADS - 1 + 3 + NZ)

    def send_keys(i, carry):
        zz, yy = to_plane(i // 4), (y + i % 4) % 4
        pltpu.make_async_remote_copy(
            src_ref=send_kv.at[zz * 4 + yy],
            dst_ref=rkv.at[z, core, x, y],
            send_sem=s_kv, recv_sem=r_kv.at[z],
            device_id=group(yy, zz), device_id_type=MESH,
        ).start()
        return carry

    def send_queries(i, carry):
        zz, yy = to_plane(i // 4), (y + i % 4) % 4
        pltpu.make_async_remote_copy(
            src_ref=send_q.at[zz * 4 + yy],
            dst_ref=rq.at[z, y],
            send_sem=s_q, recv_sem=r_q.at[z],
            device_id=group(yy, zz), device_id_type=MESH,
        ).start()
        return carry

    pltpu.make_async_copy(send_kv.at[z * 4 + y], rkv.at[z, core, x, y], r_kv.at[z]).start()
    lax.fori_loop(1, HEADS, send_keys, 0)
    pltpu.make_async_copy(send_q.at[z * 4 + y], rq.at[z, y], r_q.at[z]).start()
    lax.fori_loop(1, HEADS, send_queries, 0)

    pieces = []
    for hf in range(2):
        for pr in range(2):
            for pc in range(2):
                pieces.append(noisy_ref[pr, pl.ds(hf * 16 + pc, 8, stride=2), :])
    noisy = jnp.concatenate(pieces, axis=1)

    def wait_recv(ref, sem):
        pltpu.make_async_remote_copy(
            src_ref=ref, dst_ref=ref, send_sem=s_kv, recv_sem=sem,
            device_id=sibling, device_id_type=MESH,
        ).wait_recv()

    def wait_send(ref, sem):
        pltpu.make_async_remote_copy(
            src_ref=ref, dst_ref=ref, send_sem=sem, recv_sem=r_core.at[0],
            device_id=sibling, device_id_type=MESH,
        ).wait_send()

    xl, xr, xo = (x + 3) % NX, (x + 1) % NX, (x + 2) % NX

    def spread(i, carry):
        @pl.when(i < NZ)
        def _():
            zs = from_plane(i)
            own = rkv.at[zs, core, x]
            wait_recv(own, r_kv.at[zs])
            pltpu.make_async_remote_copy(
                src_ref=own, dst_ref=own, send_sem=s_b1, recv_sem=r_b1.at[zs, 0],
                device_id=right, device_id_type=MESH,
            ).start()
            pltpu.make_async_remote_copy(
                src_ref=own, dst_ref=own, send_sem=s_b1, recv_sem=r_b1.at[zs, 1],
                device_id=left, device_id_type=MESH,
            ).start()

        @pl.when((i >= 1) & (i < NZ + 1))
        def _():
            zs = from_plane(i - 1)
            wait_recv(rkv.at[zs, core, xl], r_b1.at[zs, 0])
            first = rkv.at[zs, core, xl, pl.ds(0, 2)]
            pltpu.make_async_remote_copy(
                src_ref=first, dst_ref=first, send_sem=s_b2, recv_sem=r_b2.at[zs, 0],
                device_id=right, device_id_type=MESH,
            ).start()
            wait_recv(rkv.at[zs, core, xr], r_b1.at[zs, 1])
            second = rkv.at[zs, core, xr, pl.ds(2, 2)]
            pltpu.make_async_remote_copy(
                src_ref=second, dst_ref=second, send_sem=s_b2, recv_sem=r_b2.at[zs, 1],
                device_id=left, device_id_type=MESH,
            ).start()

        @pl.when((i >= 2) & (i < NZ + 2))
        def _():
            zs = from_plane(i - 2)
            wait_recv(rkv.at[zs, core, xo, pl.ds(0, 2)], r_b2.at[zs, 0])
            wait_recv(rkv.at[zs, core, xo, pl.ds(2, 2)], r_b2.at[zs, 1])
            pltpu.make_async_remote_copy(
                src_ref=rkv.at[zs, core], dst_ref=rkv.at[zs, core],
                send_sem=s_core, recv_sem=r_core.at[zs],
                device_id=sibling, device_id_type=MESH,
            ).start()

        @pl.when(i >= 3)
        def _():
            zs = from_plane(i - 3)
            wait_recv(rkv.at[zs, 1 - core], r_core.at[zs])
            packed = rkv[zs, :, :, :, 32:48, :].reshape(512, 128).astype(F32)
            turned = packed.T.astype(BF16)
            vt[zs, 0:64, 0:512] = turned[0:64]
            vt[zs, 0:64, 512:1024] = turned[64:128]
            vt[zs, 64:V_ROWS, :] = jnp.ones((V_ROWS - 64, 1024), BF16)

        return carry

    lax.fori_loop(0, NZ + 3, spread, 0)

    coefficient = jnp.where(cfg == 0, guide_scale, 1.0 - guide_scale).astype(F32)

    def combine(j):
        for t in range(1, 4):
            yy = (y + t) % 4
            wait_recv(c1r.at[j, yy], r_c1.at[j, yy])
        total = c1s[j, y].astype(F32)
        for t in range(1, 4):
            total = total + c1r[j, (y + t) % 4].astype(F32)
        c2s[j] = total.reshape(2, 2, 8, 128)
        for s in range(2):
            zz = from_plane(2 * j + s)
            for t in range(2):
                cc = (cfg + t) % 2
                mine = (zz == z) & (cc == cfg)

                @pl.when(mine)
                def _():
                    c2r[cfg * NZ + z] = c2s[j, s, cc]

                @pl.when(jnp.logical_not(mine))
                def _():
                    pltpu.make_async_remote_copy(
                        src_ref=c2s.at[j, s, cc], dst_ref=c2r.at[cfg * NZ + z],
                        send_sem=s_c2, recv_sem=r_c2.at[cfg * NZ + z],
                        device_id=(seq, zz * 2 + core, cc), device_id_type=MESH,
                    ).start()

    def attend(j, carry):
        za, zb = from_plane(2 * j), from_plane(2 * j + 1)
        wait_recv(rq.at[za], r_q.at[za])
        wait_recv(rq.at[zb], r_q.at[zb])
        query = jnp.concatenate([rq[za].reshape(128, 128), rq[zb].reshape(128, 128)], axis=0)

        def block(zc, state):
            largest, acc = state
            for part in range(2):
                keys = rkv[zc, :, :, :, 16 * part:16 * part + 16, :].reshape(512, 128)
                scores = lax.dot_general(
                    keys, query, (((1,), (1,)), ((), ())), preferred_element_type=F32
                ) * LOG_SCALE
                fresh = jnp.maximum(largest, jnp.max(scores, axis=0, keepdims=True))
                factor = jnp.exp2(largest - fresh)
                probs = jnp.exp2(scores - fresh).astype(BF16)
                mixed = jnp.dot(
                    vt[zc, :, 512 * part:512 * part + 512], probs, preferred_element_type=F32
                )
                acc = acc * factor + mixed
                largest = fresh
            return largest, acc

        largest, acc = lax.fori_loop(
            0, NZ, block,
            (jnp.full((1, 256), -1e30, F32), jnp.zeros((V_ROWS, 256), F32)),
        )
        out = acc[0:64] * (coefficient / acc[64:65])
        out = out.T.reshape(16, 2, 8, 64)
        out = jnp.concatenate([out[:, 0], out[:, 1]], axis=2)
        out = out.reshape(2, 4, 16, 128).astype(BF16)
        for yy in range(4):
            c1s[j, yy] = jnp.concatenate([out[0, yy], out[1, yy]], axis=0)
        for t in range(1, 4):
            yy = (y + t) % 4
            pltpu.make_async_remote_copy(
                src_ref=c1s.at[j, yy], dst_ref=c1r.at[j, y],
                send_sem=s_c1, recv_sem=r_c1.at[j, y],
                device_id=group(yy, z), device_id_type=MESH,
            ).start()

        @pl.when(j >= 1)
        def _():
            combine(j - 1)

        return carry

    lax.fori_loop(0, 4, attend, 0)
    combine(3)

    def wait_sum(i, carry):
        @pl.when(i != cfg * NZ + z)
        def _():
            wait_recv(c2r.at[i], r_c2.at[i])

        return carry

    lax.fori_loop(0, 2 * NZ, wait_sum, 0)
    clean = noisy - level_ref[0] * jnp.sum(c2r[...], axis=0)
    halo[0, 1, 0] = clean

    def neighbours(act):
        for a in range(3):
            for dr in range(-1, 2):
                for dc in range(2):
                    if (a, dr, dc) != (0, 0, 0):
                        act(a, dr, dc)

    def send_tile(a, dr, dc):
        @pl.when((seq + a < NX * NY) & (blk + dr >= 0) & (blk + dr < 2 * NZ))
        def _():
            pltpu.make_async_remote_copy(
                src_ref=halo.at[0, 1, 0], dst_ref=halo.at[a, 1 - dr, dc],
                send_sem=s_halo.at[a, 1 - dr, dc], recv_sem=r_halo.at[a, 1 - dr, dc],
                device_id=(seq + a, blk + dr, (cfg + dc) % 2), device_id_type=MESH,
            ).start()

    neighbours(send_tile)

    for hf in range(2):
        for pr in range(2):
            for pc in range(2):
                at = hf * 64 + pr * 32 + pc * 16
                clean_ref[pr, pl.ds(hf * 16 + pc, 8, stride=2), :] = clean[:, at:at + 16]

    def wait_tile(a, dr, dc):
        @pl.when((seq - a >= 0) & (blk + dr >= 0) & (blk + dr < 2 * NZ))
        def _():
            wait_recv(halo.at[a, 1 + dr, dc], r_halo.at[a, 1 + dr, dc])

    neighbours(wait_tile)

    for a in range(3):
        for row, (tile, pr) in enumerate(((0, 1), (1, 0), (1, 1), (2, 0))):
            near = halo[a, tile, 0]
            for hf in range(2):
                for pc in range(2):
                    at = hf * 64 + pr * 32 + pc * 16
                    ext[a, row, pl.ds(1 + hf * 16 + pc, 8, stride=2), :] = near[:, at:at + 16]
            far = halo[a, tile, 1]
            before = far[7:8, 64 + pr * 32 + 16:64 + pr * 32 + 32]
            after = far[0:1, pr * 32:pr * 32 + 16]
            ext[a, row, 0:1, :] = jnp.where(cfg == 1, before, 0.0)
            ext[a, row, 33:34, :] = jnp.where(cfg == 0, after, 0.0)

    tap = 0
    for a in range(3):
        for i in range(3):
            for j in range(3):
                window = ext[2 - a, i:i + 2, j:j + 32, :]
                patches[:, 16 * tap:16 * tap + 16] = window.reshape(64, 16)
                tap += 1
    conv = jnp.dot(patches[...].astype(BF16), cw_ref[...], preferred_element_type=F32)
    normed = conv * lax.rsqrt(jnp.mean(conv * conv, axis=1, keepdims=True) + norm_eps)
    decoded_ref[...] = (normed / (1.0 + jnp.exp(-normed))).astype(BF16)

    wait_send(send_kv.at[pl.ds(0, HEADS - 1)], s_kv)
    wait_send(send_q.at[pl.ds(0, HEADS - 1)], s_q)
    wait_send(rkv.at[pl.ds(0, 2)], s_b1)
    wait_send(rkv.at[pl.ds(0, 1)], s_b2)
    wait_send(rkv.at[pl.ds(0, 4)], s_core)
    wait_send(c1s.at[:, pl.ds(0, 3)], s_c1)
    wait_send(c2r.at[pl.ds(0, 2 * NZ - 1)], s_c2)

    def wait_sent(a, dr, dc):
        @pl.when((seq + a < NX * NY) & (blk + dr >= 0) & (blk + dr < 2 * NZ))
        def _():
            wait_send(halo.at[0, 1, 0], s_halo.at[a, 1 - dr, dc])

    neighbours(wait_sent)


def local(queries, keys, values, head_weight, noisy_latent, noise_level, conv_weight):
    vmem = pl.BlockSpec(memory_space=pltpu.VMEM)
    smem = pl.BlockSpec(memory_space=pltpu.SMEM)
    dma = pltpu.SemaphoreType.DMA
    clean, decoded = pl.pallas_call(
        kernel,
        out_shape=(
            jax.ShapeDtypeStruct((2, 32, 16), F32),
            jax.ShapeDtypeStruct((64, 384), BF16),
        ),
        in_specs=[vmem, vmem, vmem, vmem, vmem, smem, vmem],
        out_specs=(vmem, vmem),
        scratch_shapes=[
            pltpu.VMEM((HEADS, KV_ROWS, 128), BF16),
            pltpu.VMEM((HEADS, ROWS, 128), BF16),
            pltpu.VMEM((NZ, 2, NX, NY, KV_ROWS, 128), BF16),
            pltpu.VMEM((NZ, NY, ROWS, 128), BF16),
            pltpu.VMEM((NZ, V_ROWS, 1024), BF16),
            pltpu.VMEM((4, NY, 32, 128), BF16),
            pltpu.VMEM((4, NY, 32, 128), BF16),
            pltpu.VMEM((4, 2, 2, 8, 128), F32),
            pltpu.VMEM((2 * NZ, 8, 128), F32),
            pltpu.VMEM((3, 3, 2, 8, 128), F32),
            pltpu.VMEM((3, 4, 40, 16), F32),
            pltpu.VMEM((64, 432), F32),
            pltpu.VMEM((8, 128), F32),
            dma, dma, dma((NZ,)), dma((NZ,)),
            dma, dma((NZ, 2)), dma, dma((NZ, 2)), dma, dma((NZ,)),
            dma, dma((4, NY)), dma, dma((2 * NZ,)), dma((3, 3, 2)), dma((3, 3, 2)),
        ],
        compiler_params=pltpu.CompilerParams(
            collective_id=0, has_side_effects=True, vmem_limit_bytes=40 * 1024 * 1024
        ),
        name="denoise",
    )(
        queries[0], keys[0], values[0], head_weight, noisy_latent[0], noise_level,
        conv_weight.reshape(432, 384),
    )
    return clean[None], decoded.reshape(1, 2, 32, 384)


def solution(mesh):
    in_specs = (
        P("cfg", ("seq", "blk"), None),
        P("cfg", ("seq", "blk"), None),
        P("cfg", ("seq", "blk"), None),
        P(),
        P("seq", "blk", "cfg", None),
        P(),
        P(),
    )
    out_specs = (P("seq", "blk", "cfg", None), P("seq", "blk", "cfg", None))
    return jax.shard_map(local, mesh=mesh, in_specs=in_specs, out_specs=out_specs, check_vma=False)
```

```python
import jax
import jax.numpy as jnp
from jax import lax
from jax.experimental import pallas as pl
from jax.experimental.pallas import tpu as pltpu
from jax.sharding import PartitionSpec as P

F32 = jnp.float32
BF16 = jnp.bfloat16
MESH = pl.DeviceIdType.MESH

guide_scale = 5.0
norm_eps = 1e-06
LOG_SCALE = float(128 ** (-0.5) * 1.4426950408889634)

NX = 4
NY = 4
NZ = 8
HEADS = 32
ROWS = 32
KV_ROWS = 48
V_ROWS = 80
TILE = 256


def kernel(
    q_hbm, k_hbm, v_hbm, wt_hbm, noisy_hbm, level_ref, cw_hbm,
    clean_ref, decoded_ref,
    q_ref, k_ref, v_ref, wt_ref, noisy_ref, cw_ref, s_load,
    send_kv, send_q, rkv, rq, vt, acc, top, c1s, c1r, c2s, c2r, noisy, halo, ext, patches, pixels,
    s_kv, s_q, r_kv, r_q, s_x, r_x, s_core, r_core,
    s_c1, r_c1, s_c2, r_c2, s_noisy, r_noisy, s_halo, r_halo,
):
    seq = lax.axis_index("seq")
    blk = lax.axis_index("blk")
    cfg = lax.axis_index("cfg")
    y, x = seq // NX, seq % NX
    z, core = blk // 2, blk % 2

    def from_plane(i):
        return (z + NZ - i) % NZ

    def group(yy, zz):
        return (yy * NX + x, zz * 2 + core, cfg)

    def target(i):
        yy, zz = (y + i % NY) % NY, (z + i // NY) % NZ
        return group(yy, zz), zz * NY + yy

    beside = [(y * NX + (x + t) % NX, blk, cfg) for t in (1, 3, 2)]
    sibling = (seq, z * 2 + 1 - core, cfg)
    partner = (seq, blk, 1 - cfg)

    def remote(src, dst, send_sem, recv_sem, device):
        return pltpu.make_async_remote_copy(
            src_ref=src, dst_ref=dst, send_sem=send_sem, recv_sem=recv_sem,
            device_id=device, device_id_type=MESH,
        )

    def wait_recv(ref, sem):
        remote(ref, ref, s_kv, sem, sibling).wait_recv()

    def wait_send(ref, sem):
        remote(ref, ref, sem, r_core.at[0], sibling).wait_send()

    loads = [
        pltpu.make_async_copy(src, dst, s_load.at[i])
        for i, (src, dst) in enumerate((
            (q_hbm, q_ref), (k_hbm, k_ref), (v_hbm, v_ref), (wt_hbm, wt_ref),
            (noisy_hbm, noisy_ref), (cw_hbm, cw_ref),
        ))
    ]
    for load in loads:
        load.start()

    halo[...] = jnp.zeros_like(halo)

    barrier = pltpu.get_barrier_semaphore()

    def greet(i, carry):
        pl.semaphore_signal(barrier, inc=1, device_id=target(i)[0], device_id_type=MESH)
        return carry

    lax.fori_loop(1, HEADS, greet, 0)
    for other in (*beside, sibling):
        pl.semaphore_signal(barrier, inc=1, device_id=other, device_id_type=MESH)

    def greet_branch(i, carry):
        pl.semaphore_signal(
            barrier, inc=1, device_id=(seq, i * 2 + core, 1 - cfg), device_id_type=MESH
        )
        return carry

    lax.fori_loop(0, NZ, greet_branch, 0)

    loads[0].wait()
    for h in range(HEADS):
        send_q[h] = q_ref[:, h * 128:(h + 1) * 128]

    loads[4].wait()
    for pr in range(2):
        pixels[pr] = noisy_ref[pr].T
    pieces = []
    for hf in range(2):
        for pr in range(2):
            for pc in range(2):
                pieces.append(pixels[pr, pl.ds(hf * 16 + pc, 8, stride=2), :])
    noisy[cfg] = jnp.concatenate(pieces, axis=1)

    pl.semaphore_wait(barrier, HEADS - 1 + NX + NZ)

    def send_queries(i, carry):
        device, head = target(i)
        remote(send_q.at[head], rq.at[y, z], s_q, r_q, device).start()
        return carry

    pltpu.make_async_copy(send_q.at[z * NY + y], rq.at[y, z], r_q).start()
    lax.fori_loop(1, HEADS, send_queries, 0)
    remote(noisy.at[cfg], noisy.at[cfg], s_noisy, r_noisy, partner).start()

    for load in loads[1:4]:
        load.wait()
    for h in range(HEADS):
        cols = slice(h * 128, (h + 1) * 128)
        send_kv[h, 0:32, :] = k_ref[:, cols]
        vp = lax.dot_general(
            v_ref[:, cols], wt_ref[:, cols], (((1,), (1,)), ((), ())), preferred_element_type=F32
        )
        send_kv[h, 32:48, :] = jnp.concatenate([vp[0:16], vp[16:32]], axis=1).astype(BF16)

    def send_keys(i, carry):
        device, head = target(i)
        remote(send_kv.at[head], rkv.at[z, core, x, y], s_kv, r_kv.at[z], device).start()
        return carry

    pltpu.make_async_copy(send_kv.at[z * NY + y], rkv.at[z, core, x, y], r_kv.at[z]).start()
    lax.fori_loop(1, HEADS, send_keys, 0)

    ext[...] = jnp.zeros_like(ext)
    acc[...] = jnp.zeros_like(acc)
    top[...] = jnp.full(top.shape, -1e30, F32)
    vt[:, 64:V_ROWS, :] = jnp.ones((NZ, V_ROWS - 64, 1024), BF16)

    coefficient = jnp.where(cfg == 0, guide_scale, 1.0 - guide_scale).astype(F32)

    def attend(zc):
        keys = jnp.concatenate(
            [rkv[zc, :, :, :, 16 * p:16 * p + 16, :].reshape(512, 128) for p in range(2)], axis=0
        )

        def scores_of(u):
            return lax.dot_general(
                keys, rq[(y + 1 + u) % NY].reshape(TILE, 128), (((1,), (1,)), ((), ())),
                preferred_element_type=F32,
            )

        scores = scores_of(0)
        for u in range(NY):
            yy = (y + 1 + u) % NY
            following = scores_of(u + 1) if u < NY - 1 else None
            before = top[yy, 0:1, :]
            fresh = jnp.maximum(before, jnp.max(scores, axis=0, keepdims=True) * LOG_SCALE)
            probs = jnp.exp2(scores * LOG_SCALE - fresh).astype(BF16)
            mixed = jnp.dot(vt[zc], probs, preferred_element_type=F32)
            acc[yy] = acc[yy] * jnp.exp2(before - fresh) + mixed
            top[yy, 0:1, :] = fresh
            scores = following

    def finish(u):
        yy = (y + 1 + u) % NY
        out = acc[yy, 0:64, :] * (coefficient / acc[yy, 64:65, :])
        out = out.T.reshape(2 * NZ, 2, 8, 64)
        out = jnp.concatenate([out[:, 0], out[:, 1]], axis=2)
        c1s[yy] = out.reshape(NZ, 16, 128).astype(BF16)
        if u < NY - 1:
            remote(c1s.at[yy], c1r.at[y], s_c1, r_c1.at[y], group(yy, z)).start()

    def step(n, carry):
        @pl.when(n < NZ)
        def _():
            zs = from_plane(n)
            own = rkv.at[zs, core, x]
            wait_recv(own, r_kv.at[zs])
            for device in beside:
                remote(own, own, s_x, r_x.at[zs, x], device).start()

        @pl.when((n >= 2) & (n < NZ + 2))
        def _():
            zs = from_plane(n - 2)
            for t in range(1, NX):
                xx = (x + t) % NX
                wait_recv(rkv.at[zs, core, xx], r_x.at[zs, xx])
            mine = rkv.at[zs, core]
            remote(mine, mine, s_core, r_core.at[zs], sibling).start()

        @pl.when(n == 3)
        def _():
            wait_recv(rq, r_q)

        @pl.when(n >= 3)
        def _():
            zs = from_plane(n - 3)
            wait_recv(rkv.at[zs, 1 - core], r_core.at[zs])
            packed = rkv[zs, :, :, :, 32:48, :].reshape(512, 128).astype(F32)
            turned = packed.T.astype(BF16)
            vt[zs, 0:64, 0:512] = turned[0:64]
            vt[zs, 0:64, 512:1024] = turned[64:128]
            attend(zs)

        return carry

    lax.fori_loop(0, NZ + 3, step, 0)
    for u in range(NY):
        finish(u)

    total = c1s[y].astype(F32)
    for t in range(1, NY):
        yy = (y + t) % NY
        wait_recv(c1r.at[yy], r_c1.at[yy])
        total = total + c1r[yy].astype(F32)
    c2s[...] = total.astype(BF16)
    c2r[cfg * NZ + z] = c2s[z]

    def send_sums(i, carry):
        zz, cc = (z + i // 2) % NZ, (cfg + i % 2) % 2
        remote(
            c2s.at[zz], c2r.at[cfg * NZ + z], s_c2, r_c2.at[cfg * NZ + z],
            (seq, zz * 2 + core, cc),
        ).start()
        return carry

    lax.fori_loop(1, 2 * NZ, send_sums, 0)
    wait_recv(noisy.at[1 - cfg], r_noisy)

    def wait_sum(i, carry):
        slot = (cfg * NZ + z + i) % (2 * NZ)
        wait_recv(c2r.at[slot], r_c2.at[slot])
        return carry

    lax.fori_loop(1, 2 * NZ, wait_sum, 0)
    velocity = jnp.sum(c2r[...].astype(F32), axis=0).reshape(2, 8, 128)
    halo[0, 1] = noisy[...] - level_ref[0] * velocity

    def neighbours(act):
        for a in range(3):
            for dr in range(-1, 2):
                if (a, dr) != (0, 0):
                    act(a, dr)

    def send_tile(a, dr):
        @pl.when((seq + a < NX * NY) & (blk + dr >= 0) & (blk + dr < 2 * NZ))
        def _():
            remote(
                halo.at[0, 1], halo.at[a, 1 - dr], s_halo.at[a, 1 - dr], r_halo.at[a, 1 - dr],
                (seq + a, blk + dr, cfg),
            ).start()

    neighbours(send_tile)
    loads[5].wait()

    def put_pixels(tile, pr, place):
        for hf in range(2):
            for pc in range(2):
                at = hf * 64 + pr * 32 + pc * 16
                place(hf * 16 + pc, tile[:, at:at + 16])

    clean = halo[0, 1, cfg]
    for pr in range(2):
        def place(start, values):
            pixels[pr, pl.ds(start, 8, stride=2), :] = values

        put_pixels(clean, pr, place)
        clean_ref[pr] = pixels[pr].T

    def wait_tile(a, dr):
        @pl.when((seq - a >= 0) & (blk + dr >= 0) & (blk + dr < 2 * NZ))
        def _():
            wait_recv(halo.at[a, 1 + dr], r_halo.at[a, 1 + dr])

    neighbours(wait_tile)

    for a in range(3):
        for row, (tile, pr) in enumerate(((0, 1), (1, 0), (1, 1), (2, 0))):
            def place(start, values):
                ext[a, row, pl.ds(1 + start, 8, stride=2), :] = values

            put_pixels(halo[a, tile, cfg], pr, place)
            far = halo[a, tile, 1 - cfg]
            before = far[7:8, 64 + pr * 32 + 16:64 + pr * 32 + 32]
            after = far[0:1, pr * 32:pr * 32 + 16]
            ext[a, row, 0:1, :] = jnp.where(cfg == 1, before, 0.0)
            ext[a, row, 33:34, :] = jnp.where(cfg == 0, after, 0.0)

    tap = 0
    for a in range(3):
        for i in range(3):
            for j in range(3):
                window = ext[2 - a, i:i + 2, j:j + 32, :]
                patches[:, 16 * tap:16 * tap + 16] = window.reshape(64, 16)
                tap += 1
    conv = jnp.dot(patches[...].astype(BF16), cw_ref[...], preferred_element_type=F32)
    normed = conv * lax.rsqrt(jnp.mean(conv * conv, axis=1, keepdims=True) + norm_eps)
    decoded_ref[...] = (normed / (1.0 + jnp.exp(-normed))).astype(BF16)

    wait_send(send_kv.at[pl.ds(0, HEADS - 1)], s_kv)
    wait_send(send_q.at[pl.ds(0, HEADS - 1)], s_q)
    wait_send(rkv.at[pl.ds(0, 3)], s_x)
    wait_send(rkv.at[pl.ds(0, 4)], s_core)
    wait_send(c1s.at[pl.ds(0, NY - 1)], s_c1)
    wait_send(c2r.at[pl.ds(0, 2 * NZ - 1)], s_c2)
    wait_send(noisy.at[0], s_noisy)

    def wait_sent(a, dr):
        @pl.when((seq + a < NX * NY) & (blk + dr >= 0) & (blk + dr < 2 * NZ))
        def _():
            wait_send(halo.at[0, 1], s_halo.at[a, 1 - dr])

    neighbours(wait_sent)


def local(queries, keys, values, head_weight, noisy_latent, noise_level, conv_weight):
    vmem = pl.BlockSpec(memory_space=pltpu.VMEM)
    hbm = pl.BlockSpec(memory_space=pltpu.HBM)
    smem = pl.BlockSpec(memory_space=pltpu.SMEM)
    dma = pltpu.SemaphoreType.DMA
    clean, decoded = pl.pallas_call(
        kernel,
        out_shape=(
            jax.ShapeDtypeStruct((2, 16, 32), F32),
            jax.ShapeDtypeStruct((64, 384), BF16),
        ),
        in_specs=[hbm, hbm, hbm, hbm, hbm, smem, hbm],
        out_specs=(vmem, vmem),
        scratch_shapes=[
            pltpu.VMEM((ROWS, HEADS * 128), BF16),
            pltpu.VMEM((ROWS, HEADS * 128), BF16),
            pltpu.VMEM((ROWS, HEADS * 128), BF16),
            pltpu.VMEM((64, HEADS * 128), BF16),
            pltpu.VMEM((2, 16, 32), F32),
            pltpu.VMEM((432, 384), BF16),
            dma((6,)),
            pltpu.VMEM((HEADS, KV_ROWS, 128), BF16),
            pltpu.VMEM((HEADS, ROWS, 128), BF16),
            pltpu.VMEM((NZ, 2, NX, NY, KV_ROWS, 128), BF16),
            pltpu.VMEM((NY, NZ, ROWS, 128), BF16),
            pltpu.VMEM((NZ, V_ROWS, 1024), BF16),
            pltpu.VMEM((NY, V_ROWS, TILE), F32),
            pltpu.VMEM((NY, 8, TILE), F32),
            pltpu.VMEM((NY, NZ, 16, 128), BF16),
            pltpu.VMEM((NY, NZ, 16, 128), BF16),
            pltpu.VMEM((NZ, 16, 128), BF16),
            pltpu.VMEM((2 * NZ, 16, 128), BF16),
            pltpu.VMEM((2, 8, 128), F32),
            pltpu.VMEM((3, 3, 2, 8, 128), F32),
            pltpu.VMEM((3, 4, 40, 16), F32),
            pltpu.VMEM((64, 432), F32),
            pltpu.VMEM((2, 32, 16), F32),
            dma, dma, dma((NZ,)), dma,
            dma, dma((NZ, NX)), dma, dma((NZ,)),
            dma, dma((NY,)), dma, dma((2 * NZ,)), dma, dma, dma((3, 3)), dma((3, 3)),
        ],
        compiler_params=pltpu.CompilerParams(
            collective_id=0, has_side_effects=True, vmem_limit_bytes=55142 * 1024
        ),
        name="denoise",
    )(
        queries[0], keys[0], values[0], head_weight.T,
        noisy_latent[0].transpose(0, 2, 1), noise_level, conv_weight.reshape(432, 384),
    )
    return clean.transpose(0, 2, 1)[None], decoded.reshape(1, 2, 32, 384)


def solution(mesh):
    in_specs = (
        P("cfg", ("seq", "blk"), None),
        P("cfg", ("seq", "blk"), None),
        P("cfg", ("seq", "blk"), None),
        P(),
        P("seq", "blk", "cfg", None),
        P(),
        P(),
    )
    out_specs = (P("seq", "blk", "cfg", None), P("seq", "blk", "cfg", None))
    return jax.shard_map(local, mesh=mesh, in_specs=in_specs, out_specs=out_specs, check_vma=False)
```

```python
import jax
import jax.numpy as jnp
from jax import lax
from jax.experimental import pallas as pl
from jax.experimental.pallas import tpu as pltpu
from jax.sharding import PartitionSpec as P

F32 = jnp.float32
BF16 = jnp.bfloat16
MESH = pl.DeviceIdType.MESH

guide_scale = 5.0
norm_eps = 1e-06
LOG_SCALE = float(128 ** (-0.5) * 1.4426950408889634)

NX = 4
NY = 4
NZ = 8
HEADS = 32
ROWS = 32
KV_ROWS = 48
V_ROWS = 80
TILE = 256
TILES = 4
UNITS = 8
LATE_STEP = 5
EARLY = 1


def kernel(
    q_hbm, k_hbm, v_hbm, wt_hbm, noisy_hbm, level_ref, cw_hbm,
    clean_ref, decoded_ref,
    q_ref, k_ref, v_ref, wt_ref, noisy_ref, cw_ref, s_load,
    send_kv, send_q, rkv, rq, vt, acc, top, c1s, c1r, c2s, c2r, noisy, halo, ext, patches, pixels,
    s_kv, s_q, r_kv, r_q, s_x, r_x, s_core, r_core,
    s_c1, r_c1, s_c2, r_c2, s_noisy, r_noisy, s_halo, r_halo,
):
    seq = lax.axis_index("seq")
    blk = lax.axis_index("blk")
    cfg = lax.axis_index("cfg")
    y, x = seq // NX, seq % NX
    z, core = blk // 2, blk % 2

    def from_plane(i):
        return (z + NZ - i) % NZ

    def group(yy, zz):
        return (yy * NX + x, zz * 2 + core, cfg)

    def target(i):
        yy, zz = (y + i % NY) % NY, (z + i // NY) % NZ
        return group(yy, zz), zz * NY + yy

    beside = [(y * NX + (x + t) % NX, blk, cfg) for t in (1, 3, 2)]
    sibling = (seq, z * 2 + 1 - core, cfg)
    partner = (seq, blk, 1 - cfg)

    def remote(src, dst, send_sem, recv_sem, device):
        return pltpu.make_async_remote_copy(
            src_ref=src, dst_ref=dst, send_sem=send_sem, recv_sem=recv_sem,
            device_id=device, device_id_type=MESH,
        )

    def wait_recv(ref, sem):
        remote(ref, ref, s_kv, sem, sibling).wait_recv()

    def wait_send(ref, sem):
        remote(ref, ref, sem, r_core.at[0], sibling).wait_send()

    loads = [
        pltpu.make_async_copy(src, dst, s_load.at[i])
        for i, (src, dst) in enumerate((
            (q_hbm, q_ref), (k_hbm, k_ref), (v_hbm, v_ref), (wt_hbm, wt_ref),
            (noisy_hbm, noisy_ref), (cw_hbm, cw_ref),
        ))
    ]
    for load in loads:
        load.start()

    halo[...] = jnp.zeros_like(halo)

    barrier = pltpu.get_barrier_semaphore()

    def greet(i, carry):
        pl.semaphore_signal(barrier, inc=1, device_id=target(i)[0], device_id_type=MESH)
        return carry

    lax.fori_loop(1, HEADS, greet, 0)
    for other in (*beside, sibling):
        pl.semaphore_signal(barrier, inc=1, device_id=other, device_id_type=MESH)

    def greet_branch(i, carry):
        pl.semaphore_signal(
            barrier, inc=1, device_id=(seq, i * 2 + core, 1 - cfg), device_id_type=MESH
        )
        return carry

    lax.fori_loop(0, NZ, greet_branch, 0)

    loads[0].wait()
    for h in range(HEADS):
        send_q[h] = q_ref[:, h * 128:(h + 1) * 128]

    loads[4].wait()
    for pr in range(2):
        pixels[pr] = noisy_ref[pr].T
    pieces = []
    for hf in range(2):
        for pr in range(2):
            for pc in range(2):
                pieces.append(pixels[pr, pl.ds(hf * 16 + pc, 8, stride=2), :])
    noisy[cfg] = jnp.concatenate(pieces, axis=1)

    pl.semaphore_wait(barrier, HEADS - 1 + NX + NZ)

    def send_queries(i, carry):
        device, head = target(i)
        at = i // NY
        remote(send_q.at[head], rq.at[at, y], s_q, r_q.at[at // 2], device).start()
        return carry

    pltpu.make_async_copy(send_q.at[z * NY + y], rq.at[0, y], r_q.at[0]).start()
    lax.fori_loop(1, 2 * EARLY * NY, send_queries, 0)
    remote(noisy.at[cfg], noisy.at[cfg], s_noisy, r_noisy, partner).start()

    for load in loads[1:4]:
        load.wait()
    for h in range(HEADS):
        cols = slice(h * 128, (h + 1) * 128)
        send_kv[h, 0:32, :] = k_ref[:, cols]
        vp = lax.dot_general(
            v_ref[:, cols], wt_ref[:, cols], (((1,), (1,)), ((), ())), preferred_element_type=F32
        )
        send_kv[h, 32:48, :] = jnp.concatenate([vp[0:16], vp[16:32]], axis=1).astype(BF16)

    def send_keys(i, carry):
        device, head = target(i)
        remote(send_kv.at[head], rkv.at[z, core, x, y], s_kv, r_kv.at[z], device).start()
        return carry

    pltpu.make_async_copy(send_kv.at[z * NY + y], rkv.at[z, core, x, y], r_kv.at[z]).start()
    lax.fori_loop(1, HEADS, send_keys, 0)

    ext[...] = jnp.zeros_like(ext)
    acc[...] = jnp.zeros_like(acc)
    top[...] = jnp.full(top.shape, -1e30, F32)
    vt[:, 64:V_ROWS, :] = jnp.ones((NZ, V_ROWS - 64, 1024), BF16)

    coefficient = jnp.where(cfg == 0, guide_scale, 1.0 - guide_scale).astype(F32)

    def attend(units):
        def scores_of(zc, t):
            keys = jnp.concatenate(
                [rkv[zc, :, :, :, 16 * p:16 * p + 16, :].reshape(512, 128) for p in range(2)], axis=0
            )
            return lax.dot_general(
                keys, rq[pl.ds(2 * t, 2)].reshape(TILE, 128), (((1,), (1,)), ((), ())),
                preferred_element_type=F32,
            )

        scores = scores_of(*units[0])
        for at, (zc, t) in enumerate(units):
            following = scores_of(*units[at + 1]) if at + 1 < len(units) else None
            before = top[t, 0:1, :]
            fresh = jnp.maximum(before, jnp.max(scores, axis=0, keepdims=True) * LOG_SCALE)
            probs = jnp.exp2(scores * LOG_SCALE - fresh).astype(BF16)
            mixed = jnp.dot(vt[zc], probs, preferred_element_type=F32)
            acc[t] = acc[t] * jnp.exp2(before - fresh) + mixed
            top[t, 0:1, :] = fresh
            scores = following

    def finish(t):
        out = acc[t, 0:64, :] * (coefficient / acc[t, 64:65, :])
        out = out.T.reshape(16, 2, 8, 64)
        out = jnp.concatenate([out[:, 0], out[:, 1]], axis=2)
        out = out.reshape(2, NY, 16, 128).astype(BF16)
        for yy in range(NY):
            c1s[yy, pl.ds(2 * t, 2)] = out[:, yy]
        for dy in range(1, NY):
            yy = (y + dy) % NY
            remote(
                c1s.at[yy, pl.ds(2 * t, 2)], c1r.at[y, pl.ds(2 * t, 2)],
                s_c1, r_c1.at[t, y], group(yy, z),
            ).start()

    def combine(t):
        total = c1s[y, pl.ds(2 * t, 2)].astype(F32)
        for dy in range(1, NY):
            yy = (y + dy) % NY
            wait_recv(c1r.at[yy, pl.ds(2 * t, 2)], r_c1.at[t, yy])
            total = total + c1r[yy, pl.ds(2 * t, 2)].astype(F32)
        c2s[pl.ds(2 * t, 2)] = total.astype(BF16)
        for s in range(2):
            i = 2 * t + s
            zz = from_plane(i)

            def send(cc):
                remote(
                    c2s.at[i], c2r.at[cfg * NZ + z], s_c2, r_c2.at[cfg * NZ + z],
                    (seq, zz * 2 + core, cc),
                ).start()

            send(1 - cfg)

            @pl.when(i > 0)
            def _():
                send(cfg)

            @pl.when(i == 0)
            def _():
                c2r[cfg * NZ + z] = c2s[0]

    def take(zs):
        wait_recv(rkv.at[zs, 1 - core], r_core.at[zs])
        packed = rkv[zs, :, :, :, 32:48, :].reshape(512, 128).astype(F32)
        turned = packed.T.astype(BF16)
        vt[zs, 0:64, 0:512] = turned[0:64]
        vt[zs, 0:64, 512:1024] = turned[64:128]

    def share(zs):
        for t in range(1, NX):
            xx = (x + t) % NX
            wait_recv(rkv.at[zs, core, xx], r_x.at[zs, xx])
        mine = rkv.at[zs, core]
        remote(mine, mine, s_core, r_core.at[zs], sibling).start()

    def wait_queries(tiles):
        for t in tiles:
            wait_recv(rq.at[pl.ds(2 * t, 2)], r_q.at[t])

    def step(n, carry):
        @pl.when(n < NZ)
        def _():
            zs = from_plane(n)
            own = rkv.at[zs, core, x]
            wait_recv(own, r_kv.at[zs])
            for device in beside:
                remote(own, own, s_x, r_x.at[zs, x], device).start()

        @pl.when((n >= LATE_STEP) & (n < LATE_STEP + TILES - EARLY))
        def _():
            first = (n - LATE_STEP + EARLY) * 2 * NY
            lax.fori_loop(first, first + 2 * NY, send_queries, 0)

        @pl.when((n >= 2) & (n < NZ + 2))
        def _():
            share(from_plane(n - 2))

        @pl.when(n == 3)
        def _():
            wait_queries(range(EARLY))

        @pl.when(n >= 3)
        def _():
            zs = from_plane(n - 3)
            take(zs)
            attend([(zs, t) for t in range(EARLY)])

        return carry

    lax.fori_loop(0, NZ + 3, step, 0)
    for t in range(EARLY):
        finish(t)

    def late(t, carry):
        wait_recv(rq.at[pl.ds(2 * t, 2)], r_q.at[t])

        def chunks(k, inner):
            attend([(UNITS * k + u, t) for u in range(UNITS)])
            return inner

        lax.fori_loop(0, NZ // UNITS, chunks, 0)
        finish(t)
        combine(t - EARLY)
        return carry

    lax.fori_loop(EARLY, TILES, late, 0)
    for t in range(TILES - EARLY, TILES):
        combine(t)

    wait_recv(noisy.at[1 - cfg], r_noisy)

    def wait_sum(i, carry):
        slot = (cfg * NZ + z + i) % (2 * NZ)
        wait_recv(c2r.at[slot], r_c2.at[slot])
        return carry

    lax.fori_loop(1, 2 * NZ, wait_sum, 0)
    velocity = jnp.sum(c2r[...].astype(F32), axis=0).reshape(2, 8, 128)
    halo[0, 1] = noisy[...] - level_ref[0] * velocity

    def neighbours(act):
        for a in range(3):
            for dr in range(-1, 2):
                if (a, dr) != (0, 0):
                    act(a, dr)

    def send_tile(a, dr):
        @pl.when((seq + a < NX * NY) & (blk + dr >= 0) & (blk + dr < 2 * NZ))
        def _():
            remote(
                halo.at[0, 1], halo.at[a, 1 - dr], s_halo.at[a, 1 - dr], r_halo.at[a, 1 - dr],
                (seq + a, blk + dr, cfg),
            ).start()

    neighbours(send_tile)
    loads[5].wait()

    def put_pixels(tile, pr, place):
        for hf in range(2):
            for pc in range(2):
                at = hf * 64 + pr * 32 + pc * 16
                place(hf * 16 + pc, tile[:, at:at + 16])

    clean = halo[0, 1, cfg]
    for pr in range(2):
        def place(start, values):
            pixels[pr, pl.ds(start, 8, stride=2), :] = values

        put_pixels(clean, pr, place)
        clean_ref[pr] = pixels[pr].T

    def wait_tile(a, dr):
        @pl.when((seq - a >= 0) & (blk + dr >= 0) & (blk + dr < 2 * NZ))
        def _():
            wait_recv(halo.at[a, 1 + dr], r_halo.at[a, 1 + dr])

    neighbours(wait_tile)

    for a in range(3):
        for row, (tile, pr) in enumerate(((0, 1), (1, 0), (1, 1), (2, 0))):
            def place(start, values):
                ext[a, row, pl.ds(1 + start, 8, stride=2), :] = values

            put_pixels(halo[a, tile, cfg], pr, place)
            far = halo[a, tile, 1 - cfg]
            before = far[7:8, 64 + pr * 32 + 16:64 + pr * 32 + 32]
            after = far[0:1, pr * 32:pr * 32 + 16]
            ext[a, row, 0:1, :] = jnp.where(cfg == 1, before, 0.0)
            ext[a, row, 33:34, :] = jnp.where(cfg == 0, after, 0.0)

    tap = 0
    for a in range(3):
        for i in range(3):
            for j in range(3):
                window = ext[2 - a, i:i + 2, j:j + 32, :]
                patches[:, 16 * tap:16 * tap + 16] = window.reshape(64, 16)
                tap += 1
    conv = jnp.dot(patches[...].astype(BF16), cw_ref[...], preferred_element_type=F32)
    normed = conv * lax.rsqrt(jnp.mean(conv * conv, axis=1, keepdims=True) + norm_eps)
    decoded_ref[...] = (normed / (1.0 + jnp.exp(-normed))).astype(BF16)

    wait_send(send_kv.at[pl.ds(0, HEADS - 1)], s_kv)
    wait_send(send_q.at[pl.ds(0, HEADS - 1)], s_q)
    wait_send(rkv.at[pl.ds(0, 3)], s_x)
    wait_send(rkv.at[pl.ds(0, 4)], s_core)
    wait_send(c1s.at[pl.ds(0, NY - 1)], s_c1)
    wait_send(c2r.at[pl.ds(0, 2 * NZ - 1)], s_c2)
    wait_send(noisy.at[0], s_noisy)

    def wait_sent(a, dr):
        @pl.when((seq + a < NX * NY) & (blk + dr >= 0) & (blk + dr < 2 * NZ))
        def _():
            wait_send(halo.at[0, 1], s_halo.at[a, 1 - dr])

    neighbours(wait_sent)


def local(queries, keys, values, head_weight, noisy_latent, noise_level, conv_weight):
    vmem = pl.BlockSpec(memory_space=pltpu.VMEM)
    hbm = pl.BlockSpec(memory_space=pltpu.HBM)
    smem = pl.BlockSpec(memory_space=pltpu.SMEM)
    dma = pltpu.SemaphoreType.DMA
    clean, decoded = pl.pallas_call(
        kernel,
        out_shape=(
            jax.ShapeDtypeStruct((2, 16, 32), F32),
            jax.ShapeDtypeStruct((64, 384), BF16),
        ),
        in_specs=[hbm, hbm, hbm, hbm, hbm, smem, hbm],
        out_specs=(vmem, vmem),
        scratch_shapes=[
            pltpu.VMEM((ROWS, HEADS * 128), BF16),
            pltpu.VMEM((ROWS, HEADS * 128), BF16),
            pltpu.VMEM((ROWS, HEADS * 128), BF16),
            pltpu.VMEM((64, HEADS * 128), BF16),
            pltpu.VMEM((2, 16, 32), F32),
            pltpu.VMEM((432, 384), BF16),
            dma((6,)),
            pltpu.VMEM((HEADS, KV_ROWS, 128), BF16),
            pltpu.VMEM((HEADS, ROWS, 128), BF16),
            pltpu.VMEM((NZ, 2, NX, NY, KV_ROWS, 128), BF16),
            pltpu.VMEM((NZ, NY, ROWS, 128), BF16),
            pltpu.VMEM((NZ, V_ROWS, 1024), BF16),
            pltpu.VMEM((TILES, V_ROWS, TILE), F32),
            pltpu.VMEM((TILES, 8, TILE), F32),
            pltpu.VMEM((NY, NZ, 16, 128), BF16),
            pltpu.VMEM((NY, NZ, 16, 128), BF16),
            pltpu.VMEM((NZ, 16, 128), BF16),
            pltpu.VMEM((2 * NZ, 16, 128), BF16),
            pltpu.VMEM((2, 8, 128), F32),
            pltpu.VMEM((3, 3, 2, 8, 128), F32),
            pltpu.VMEM((3, 4, 40, 16), F32),
            pltpu.VMEM((64, 432), F32),
            pltpu.VMEM((2, 32, 16), F32),
            dma, dma, dma((NZ,)), dma((TILES,)),
            dma, dma((NZ, NX)), dma, dma((NZ,)),
            dma, dma((TILES, NY)), dma, dma((2 * NZ,)), dma, dma, dma((3, 3)), dma((3, 3)),
        ],
        compiler_params=pltpu.CompilerParams(
            collective_id=0, has_side_effects=True, vmem_limit_bytes=55142 * 1024
        ),
        name="denoise",
    )(
        queries[0], keys[0], values[0], head_weight.T,
        noisy_latent[0].transpose(0, 2, 1), noise_level, conv_weight.reshape(432, 384),
    )
    return clean.transpose(0, 2, 1)[None], decoded.reshape(1, 2, 32, 384)


def solution(mesh):
    in_specs = (
        P("cfg", ("seq", "blk"), None),
        P("cfg", ("seq", "blk"), None),
        P("cfg", ("seq", "blk"), None),
        P(),
        P("seq", "blk", "cfg", None),
        P(),
        P(),
    )
    out_specs = (P("seq", "blk", "cfg", None), P("seq", "blk", "cfg", None))
    return jax.shard_map(local, mesh=mesh, in_specs=in_specs, out_specs=out_specs, check_vma=False)
```

```python
import jax
import jax.numpy as jnp
from jax import lax
from jax.experimental import pallas as pl
from jax.experimental.pallas import tpu as pltpu
from jax.sharding import PartitionSpec as P

F32 = jnp.float32
BF16 = jnp.bfloat16
MESH = pl.DeviceIdType.MESH

guide_scale = 5.0
norm_eps = 1e-06
LOG_SCALE = float(128 ** (-0.5) * 1.4426950408889634)

NX = 4
NY = 4
NZ = 8
HEADS = 32
ROWS = 32
KV_ROWS = 48
V_ROWS = 80
TILE = 256
TILES = 4
LATE_STEP = 5
EARLY = 1


def kernel(
    q_hbm, k_hbm, v_hbm, wt_hbm, noisy_hbm, level_ref, cw_hbm,
    clean_ref, decoded_ref,
    q_ref, k_ref, v_ref, wt_ref, noisy_ref, cw_ref, s_load,
    send_kv, send_q, rkv, rq, vt, acc, top, c1s, c1r, c2s, c2r, noisy, halo, ext, patches, pixels,
    s_kv, s_q, r_kv, r_q, s_x, r_x, s_core, r_core,
    s_c1, r_c1, s_c2, r_c2, s_noisy, r_noisy, s_halo, r_halo,
):
    seq = lax.axis_index("seq")
    blk = lax.axis_index("blk")
    cfg = lax.axis_index("cfg")
    y, x = seq // NX, seq % NX
    z, core = blk // 2, blk % 2

    def from_plane(i):
        return (z + NZ - i) % NZ

    def group(yy, zz):
        return (yy * NX + x, zz * 2 + core, cfg)

    def target(i):
        yy, zz = (y + i % NY) % NY, (z + i // NY) % NZ
        return group(yy, zz), zz * NY + yy

    beside = [(y * NX + (x + t) % NX, blk, cfg) for t in (1, 3, 2)]
    sibling = (seq, z * 2 + 1 - core, cfg)
    partner = (seq, blk, 1 - cfg)

    def remote(src, dst, send_sem, recv_sem, device):
        return pltpu.make_async_remote_copy(
            src_ref=src, dst_ref=dst, send_sem=send_sem, recv_sem=recv_sem,
            device_id=device, device_id_type=MESH,
        )

    def wait_recv(ref, sem):
        remote(ref, ref, s_kv, sem, sibling).wait_recv()

    def wait_send(ref, sem):
        remote(ref, ref, sem, r_core.at[0], sibling).wait_send()

    loads = [
        pltpu.make_async_copy(src, dst, s_load.at[i])
        for i, (src, dst) in enumerate((
            (q_hbm, q_ref), (k_hbm, k_ref), (v_hbm, v_ref), (wt_hbm, wt_ref),
            (noisy_hbm, noisy_ref), (cw_hbm, cw_ref),
        ))
    ]
    for load in loads:
        load.start()

    halo[...] = jnp.zeros_like(halo)

    barrier = pltpu.get_barrier_semaphore()

    def greet(i, carry):
        pl.semaphore_signal(barrier, inc=1, device_id=target(i)[0], device_id_type=MESH)
        return carry

    lax.fori_loop(1, HEADS, greet, 0)
    for other in (*beside, sibling):
        pl.semaphore_signal(barrier, inc=1, device_id=other, device_id_type=MESH)

    def greet_branch(i, carry):
        pl.semaphore_signal(
            barrier, inc=1, device_id=(seq, i * 2 + core, 1 - cfg), device_id_type=MESH
        )
        return carry

    lax.fori_loop(0, NZ, greet_branch, 0)

    loads[0].wait()
    for h in range(HEADS):
        send_q[h] = q_ref[:, h * 128:(h + 1) * 128]

    loads[4].wait()
    for pr in range(2):
        pixels[pr] = noisy_ref[pr].T
    pieces = []
    for hf in range(2):
        for pr in range(2):
            for pc in range(2):
                pieces.append(pixels[pr, pl.ds(hf * 16 + pc, 8, stride=2), :])
    noisy[cfg] = jnp.concatenate(pieces, axis=1)

    pl.semaphore_wait(barrier, HEADS - 1 + NX + NZ)

    def send_queries(i, carry):
        device, head = target(i)
        at = i // NY
        remote(send_q.at[head], rq.at[at, y], s_q, r_q.at[at // 2], device).start()
        return carry

    pltpu.make_async_copy(send_q.at[z * NY + y], rq.at[0, y], r_q.at[0]).start()
    lax.fori_loop(1, 2 * EARLY * NY, send_queries, 0)
    remote(noisy.at[cfg], noisy.at[cfg], s_noisy, r_noisy, partner).start()

    for load in loads[1:4]:
        load.wait()
    for h in range(HEADS):
        cols = slice(h * 128, (h + 1) * 128)
        send_kv[h, 0:32, :] = k_ref[:, cols]
        vp = lax.dot_general(
            v_ref[:, cols], wt_ref[:, cols], (((1,), (1,)), ((), ())), preferred_element_type=F32
        )
        send_kv[h, 32:48, :] = jnp.concatenate([vp[0:16], vp[16:32]], axis=1).astype(BF16)

    def send_keys(i, carry):
        device, head = target(i)
        remote(send_kv.at[head], rkv.at[z, core, x, y], s_kv, r_kv.at[z], device).start()
        return carry

    pltpu.make_async_copy(send_kv.at[z * NY + y], rkv.at[z, core, x, y], r_kv.at[z]).start()
    lax.fori_loop(1, HEADS, send_keys, 0)

    ext[...] = jnp.zeros_like(ext)
    acc[...] = jnp.zeros_like(acc)
    top[...] = jnp.full(top.shape, -1e30, F32)
    vt[:, 64:V_ROWS, :] = jnp.ones((NZ, V_ROWS - 64, 1024), BF16)

    coefficient = jnp.where(cfg == 0, guide_scale, 1.0 - guide_scale).astype(F32)

    def attend(units):
        def scores_of(zc, t):
            keys = jnp.concatenate(
                [rkv[zc, :, :, :, 16 * p:16 * p + 16, :].reshape(512, 128) for p in range(2)], axis=0
            )
            return lax.dot_general(
                keys, rq[pl.ds(2 * t, 2)].reshape(TILE, 128), (((1,), (1,)), ((), ())),
                preferred_element_type=F32,
            )

        scores = scores_of(*units[0])
        for at, (zc, t) in enumerate(units):
            following = scores_of(*units[at + 1]) if at + 1 < len(units) else None
            before = top[t, 0:1, :]
            fresh = jnp.maximum(before, jnp.max(scores, axis=0, keepdims=True) * LOG_SCALE)
            probs = jnp.exp2(scores * LOG_SCALE - fresh).astype(BF16)
            mixed = jnp.dot(vt[zc], probs, preferred_element_type=F32)
            acc[t] = acc[t] * jnp.exp2(before - fresh) + mixed
            top[t, 0:1, :] = fresh
            scores = following

    def finish(t):
        out = acc[t, 0:64, :] * (coefficient / acc[t, 64:65, :])
        out = out.T.reshape(16, 2, 8, 64)
        out = jnp.concatenate([out[:, 0], out[:, 1]], axis=2)
        out = out.reshape(2, NY, 16, 128).astype(BF16)
        for yy in range(NY):
            c1s[yy, pl.ds(2 * t, 2)] = out[:, yy]
        for dy in range(1, NY):
            yy = (y + dy) % NY
            remote(
                c1s.at[yy, pl.ds(2 * t, 2)], c1r.at[y, pl.ds(2 * t, 2)],
                s_c1, r_c1.at[t, y], group(yy, z),
            ).start()

    def combine(t):
        total = c1s[y, pl.ds(2 * t, 2)].astype(F32)
        for dy in range(1, NY):
            yy = (y + dy) % NY
            wait_recv(c1r.at[yy, pl.ds(2 * t, 2)], r_c1.at[t, yy])
            total = total + c1r[yy, pl.ds(2 * t, 2)].astype(F32)
        c2s[pl.ds(2 * t, 2)] = total.astype(BF16)
        for s in range(2):
            i = 2 * t + s
            zz = from_plane(i)

            def send(cc):
                remote(
                    c2s.at[i], c2r.at[cfg * NZ + z], s_c2, r_c2.at[cfg * NZ + z],
                    (seq, zz * 2 + core, cc),
                ).start()

            send(1 - cfg)

            @pl.when(i > 0)
            def _():
                send(cfg)

            @pl.when(i == 0)
            def _():
                c2r[cfg * NZ + z] = c2s[0]

    def take(zs):
        wait_recv(rkv.at[zs, 1 - core], r_core.at[zs])
        packed = rkv[zs, :, :, :, 32:48, :].reshape(512, 128).astype(F32)
        turned = packed.T.astype(BF16)
        vt[zs, 0:64, 0:512] = turned[0:64]
        vt[zs, 0:64, 512:1024] = turned[64:128]

    def share(zs):
        for t in range(1, NX):
            xx = (x + t) % NX
            wait_recv(rkv.at[zs, core, xx], r_x.at[zs, xx])
        mine = rkv.at[zs, core]
        remote(mine, mine, s_core, r_core.at[zs], sibling).start()

    def wait_queries(tiles):
        for t in tiles:
            wait_recv(rq.at[pl.ds(2 * t, 2)], r_q.at[t])

    def step(n, carry):
        @pl.when(n < NZ)
        def _():
            zs = from_plane(n)
            own = rkv.at[zs, core, x]
            wait_recv(own, r_kv.at[zs])
            for device in beside:
                remote(own, own, s_x, r_x.at[zs, x], device).start()

        @pl.when((n >= LATE_STEP) & (n < LATE_STEP + TILES - EARLY))
        def _():
            first = (n - LATE_STEP + EARLY) * 2 * NY
            lax.fori_loop(first, first + 2 * NY, send_queries, 0)

        @pl.when((n >= 2) & (n < NZ + 2))
        def _():
            share(from_plane(n - 2))

        @pl.when(n == 3)
        def _():
            wait_queries(range(EARLY))

        @pl.when(n >= 3)
        def _():
            zs = from_plane(n - 3)
            take(zs)
            attend([(zs, t) for t in range(EARLY)])

        return carry

    lax.fori_loop(0, NZ + 2, step, 0)

    wait_queries([1])
    attend([(from_plane(k), 1) for k in range(NZ - 1)])
    take(from_plane(NZ - 1))
    attend([(from_plane(NZ - 1), 0), (from_plane(NZ - 1), 1)])
    finish(0)
    finish(1)

    def late(t, carry):
        wait_recv(rq.at[pl.ds(2 * t, 2)], r_q.at[t])
        attend([(k, t) for k in range(NZ)])
        finish(t)
        return carry

    lax.fori_loop(2, TILES, late, 0)
    for t in range(TILES):
        combine(t)

    wait_recv(noisy.at[1 - cfg], r_noisy)

    def wait_sum(i, carry):
        slot = (cfg * NZ + z + i) % (2 * NZ)
        wait_recv(c2r.at[slot], r_c2.at[slot])
        return carry

    lax.fori_loop(1, 2 * NZ, wait_sum, 0)
    velocity = jnp.sum(c2r[...].astype(F32), axis=0).reshape(2, 8, 128)
    halo[0, 1] = noisy[...] - level_ref[0] * velocity

    def neighbours(act):
        for a in range(3):
            for dr in range(-1, 2):
                if (a, dr) != (0, 0):
                    act(a, dr)

    def send_tile(a, dr):
        @pl.when((seq + a < NX * NY) & (blk + dr >= 0) & (blk + dr < 2 * NZ))
        def _():
            remote(
                halo.at[0, 1], halo.at[a, 1 - dr], s_halo.at[a, 1 - dr], r_halo.at[a, 1 - dr],
                (seq + a, blk + dr, cfg),
            ).start()

    neighbours(send_tile)
    loads[5].wait()

    def put_pixels(tile, pr, place):
        for hf in range(2):
            for pc in range(2):
                at = hf * 64 + pr * 32 + pc * 16
                place(hf * 16 + pc, tile[:, at:at + 16])

    clean = halo[0, 1, cfg]
    for pr in range(2):
        def place(start, values):
            pixels[pr, pl.ds(start, 8, stride=2), :] = values

        put_pixels(clean, pr, place)
        clean_ref[pr] = pixels[pr].T

    def wait_tile(a, dr):
        @pl.when((seq - a >= 0) & (blk + dr >= 0) & (blk + dr < 2 * NZ))
        def _():
            wait_recv(halo.at[a, 1 + dr], r_halo.at[a, 1 + dr])

    neighbours(wait_tile)

    for a in range(3):
        for row, (tile, pr) in enumerate(((0, 1), (1, 0), (1, 1), (2, 0))):
            def place(start, values):
                ext[a, row, pl.ds(1 + start, 8, stride=2), :] = values

            put_pixels(halo[a, tile, cfg], pr, place)
            far = halo[a, tile, 1 - cfg]
            before = far[7:8, 64 + pr * 32 + 16:64 + pr * 32 + 32]
            after = far[0:1, pr * 32:pr * 32 + 16]
            ext[a, row, 0:1, :] = jnp.where(cfg == 1, before, 0.0)
            ext[a, row, 33:34, :] = jnp.where(cfg == 0, after, 0.0)

    tap = 0
    for a in range(3):
        for i in range(3):
            for j in range(3):
                window = ext[2 - a, i:i + 2, j:j + 32, :]
                patches[:, 16 * tap:16 * tap + 16] = window.reshape(64, 16)
                tap += 1
    conv = jnp.dot(patches[...].astype(BF16), cw_ref[...], preferred_element_type=F32)
    normed = conv * lax.rsqrt(jnp.mean(conv * conv, axis=1, keepdims=True) + norm_eps)
    decoded_ref[...] = (normed / (1.0 + jnp.exp(-normed))).astype(BF16)

    wait_send(send_kv.at[pl.ds(0, HEADS - 1)], s_kv)
    wait_send(send_q.at[pl.ds(0, HEADS - 1)], s_q)
    wait_send(rkv.at[pl.ds(0, 3)], s_x)
    wait_send(rkv.at[pl.ds(0, 4)], s_core)
    wait_send(c1s.at[pl.ds(0, NY - 1)], s_c1)
    wait_send(c2r.at[pl.ds(0, 2 * NZ - 1)], s_c2)
    wait_send(noisy.at[0], s_noisy)

    def wait_sent(a, dr):
        @pl.when((seq + a < NX * NY) & (blk + dr >= 0) & (blk + dr < 2 * NZ))
        def _():
            wait_send(halo.at[0, 1], s_halo.at[a, 1 - dr])

    neighbours(wait_sent)


def local(queries, keys, values, head_weight, noisy_latent, noise_level, conv_weight):
    vmem = pl.BlockSpec(memory_space=pltpu.VMEM)
    hbm = pl.BlockSpec(memory_space=pltpu.HBM)
    smem = pl.BlockSpec(memory_space=pltpu.SMEM)
    dma = pltpu.SemaphoreType.DMA
    clean, decoded = pl.pallas_call(
        kernel,
        out_shape=(
            jax.ShapeDtypeStruct((2, 16, 32), F32),
            jax.ShapeDtypeStruct((64, 384), BF16),
        ),
        in_specs=[hbm, hbm, hbm, hbm, hbm, smem, hbm],
        out_specs=(vmem, vmem),
        scratch_shapes=[
            pltpu.VMEM((ROWS, HEADS * 128), BF16),
            pltpu.VMEM((ROWS, HEADS * 128), BF16),
            pltpu.VMEM((ROWS, HEADS * 128), BF16),
            pltpu.VMEM((64, HEADS * 128), BF16),
            pltpu.VMEM((2, 16, 32), F32),
            pltpu.VMEM((432, 384), BF16),
            dma((6,)),
            pltpu.VMEM((HEADS, KV_ROWS, 128), BF16),
            pltpu.VMEM((HEADS, ROWS, 128), BF16),
            pltpu.VMEM((NZ, 2, NX, NY, KV_ROWS, 128), BF16),
            pltpu.VMEM((NZ, NY, ROWS, 128), BF16),
            pltpu.VMEM((NZ, V_ROWS, 1024), BF16),
            pltpu.VMEM((TILES, V_ROWS, TILE), F32),
            pltpu.VMEM((TILES, 8, TILE), F32),
            pltpu.VMEM((NY, NZ, 16, 128), BF16),
            pltpu.VMEM((NY, NZ, 16, 128), BF16),
            pltpu.VMEM((NZ, 16, 128), BF16),
            pltpu.VMEM((2 * NZ, 16, 128), BF16),
            pltpu.VMEM((2, 8, 128), F32),
            pltpu.VMEM((3, 3, 2, 8, 128), F32),
            pltpu.VMEM((3, 4, 40, 16), F32),
            pltpu.VMEM((64, 432), F32),
            pltpu.VMEM((2, 32, 16), F32),
            dma, dma, dma((NZ,)), dma((TILES,)),
            dma, dma((NZ, NX)), dma, dma((NZ,)),
            dma, dma((TILES, NY)), dma, dma((2 * NZ,)), dma, dma, dma((3, 3)), dma((3, 3)),
        ],
        compiler_params=pltpu.CompilerParams(
            collective_id=0, has_side_effects=True, vmem_limit_bytes=55142 * 1024
        ),
        name="denoise",
    )(
        queries[0], keys[0], values[0], head_weight.T,
        noisy_latent[0].transpose(0, 2, 1), noise_level, conv_weight.reshape(432, 384),
    )
    return clean.transpose(0, 2, 1)[None], decoded.reshape(1, 2, 32, 384)


def solution(mesh):
    in_specs = (
        P("cfg", ("seq", "blk"), None),
        P("cfg", ("seq", "blk"), None),
        P("cfg", ("seq", "blk"), None),
        P(),
        P("seq", "blk", "cfg", None),
        P(),
        P(),
    )
    out_specs = (P("seq", "blk", "cfg", None), P("seq", "blk", "cfg", None))
    return jax.shard_map(local, mesh=mesh, in_specs=in_specs, out_specs=out_specs, check_vma=False)
```
